128 devices in a mesh: gx: 8 (over y, core), gy: 16 (over x, z).
Axes of the slice: x: 4, y: 4, z: 4, core: 2. Of those that a mesh axis runs over, the one named last changes fastest.
Arguments:
- adjoint_start: float32 [2, 1024, 4096], P(None, 'gx', 'gy'), may hold values from -4 to 4
- velocity: float32 [2, 1024, 4096], P(None, 'gx', 'gy'), may hold values from -6 to 6
- viscosity: float32 [1024, 4096], P('gx', 'gy'), may hold values from 0.1 to 1
- friction: float32 [1024, 4096], P('gx', 'gy'), may hold values from 0.1 to 2
- ice_mask: int32 [1024, 4096], P('gx', 'gy'), may hold values 0 or 1
- misfit: float32 [65536, 128], P(('gx', 'gy')), may hold values from -6 to 6
- heading: float32 [65536], P(('gx', 'gy')), may hold values from -3.140625 to 3.140625
- row_dest: int32 [65536, 1], P(('gx', 'gy')), may hold values from 0 to 127; in each aligned block of 512 rows (0 to 511, 512 to 1023, ...) at most 8 rows name the same one
- live_rows: int32 [128], P(('gx', 'gy')), may hold values from 384 to 512
- pixel_lists: int32 [16384, 8, 2, 128], P(('gx', 'gy')), may hold values from 0 to 255, as said below
Outputs:
- adjoint: float32 [2, 1024, 4096], P(None, 'gx', 'gy')
- friction_gradient: float32 [1024, 4096], P('gx', 'gy')
The draws below stay inside these ranges and needn't reach their ends.
Inputs may be any that keep to these rules, and one draw needn't show every extreme that they name: `row_dest`: among the 512 rows of one device no tile is named more than 8 times. `pixel_lists`: entry 0 is a local row below 128, entry 1 a local column below 256.
All inputs are finite; a program needn't handle non-finite values. No bound on the sum of `ice_mask` on one device may be relied on, other than what follows from the above.
Results may differ from the reference program's by a relative error of at most 0.0003.
Values sent between devices are 32-bit elements; how exact they have to be, the bound alone decides.
A program may use at most 64 MiB of HBM per device.

```python
import math
import jax
import jax.numpy as jnp
import numpy as np

TX = 128
TY = 256
ROWS_DEV = 512
BLOCK = 128
ITERS = 4
TILES = 128
SLOTS = 8
NX = 1024
NY = 4096
ROWS = 65536
N_GY = 16


def draw_live_rows(key, part):
    first_key, second_key = jax.random.split(key)
    lowest = 3 * ROWS_DEV // 4
    counts = jax.random.randint(first_key, (TILES,), lowest, ROWS_DEV + 1)
    order = jax.random.permutation(second_key, TILES)
    counts = counts.at[order[0]].set(ROWS_DEV)
    counts = counts.at[order[1]].set(lowest)
    return counts.astype(jnp.int32)


def draw_pixel_lists(key, part):
    row_key = jax.random.fold_in(key, 11)
    col_key = jax.random.fold_in(key, 23)
    rows_part = jax.random.randint(row_key, (TILES * TILES, SLOTS, 1, BLOCK), 0, TX)
    cols_part = jax.random.randint(col_key, (TILES * TILES, SLOTS, 1, BLOCK), 0, TY)
    lists = jnp.concatenate([rows_part, cols_part], axis=2)
    lists = lists.at[0, 0, 0, 0].set(TX - 1)
    lists = lists.at[0, 0, 1, 0].set(TY - 1)
    return lists.astype(jnp.int32)


def place_ends(drawn, rng, least, top_value):
    longest = drawn.shape.index(max(drawn.shape))
    spots = []
    for shift in (0, 1):
        where = [jax.random.randint(jax.random.fold_in(rng, axis), (), 0, length) for axis, length in enumerate(drawn.shape)]
        where[longest] = (where[longest] + shift) % drawn.shape[longest]
        spots.append(tuple(where))
    return drawn.at[spots[0]].set(least).at[spots[1]].set(top_value)


def levels(own_key, dims, pieces, least, high):
    loudness = 1.0
    for position, shards_of in pieces:
        draws = jax.random.uniform(jax.random.fold_in(jax.random.fold_in(own_key, 6), position), (shards_of,), jnp.float32, least / len(pieces), high / len(pieces))
        loudness = loudness * jnp.repeat(jnp.exp(draws), dims[position] // shards_of).reshape((-1,) + (1,) * (len(dims) - 1 - position))
    return loudness


def shared_out(stream_key, own, number, rows, count, top, bound, lean):
    sequence = jax.random.permutation(stream_key, count)
    heavy_load, ordinary = shares(count, rows * top, bound, lean, True), shares(count, rows * top, bound, lean, False)
    places = jnp.arange(count)

    def named(sizes, offset_by):
        used = int((sizes > 0).sum())
        fixed = max(1, used // 4)
        moved = fixed + (places - fixed + offset_by * (used - fixed)) % max(1, count - fixed)
        return jnp.zeros((count,), jnp.int32).at[sequence[jnp.where(places < fixed, places, moved)]].set(jnp.asarray(sizes, jnp.int32))

    sizes = jnp.where(number % 4 == 0, named(heavy_load, number // 4), named(ordinary, number - number // 4 - 1))
    mixed = jax.random.permutation(jax.random.fold_in(own, 3), count)
    donor, sink = mixed[0:count // 2 * 2:2], mixed[1:count // 2 * 2:2]
    room = jnp.minimum(sizes[donor] - 1, bound - sizes[sink]) // 2
    room = jnp.where((donor == sequence[0]) | (sink == sequence[0]) | (sizes[sink] == 0), 0, jnp.maximum(room, 0))
    moved = jax.random.randint(jax.random.fold_in(own, 4), (count // 2,), 0, 1 << 20) % (room + 1)
    sizes = sizes.at[donor].add(-moved).at[sink].add(moved)
    items = jnp.searchsorted(jnp.cumsum(sizes), jnp.arange(rows * top), side="right").astype(jnp.int32)
    table = items.reshape(top, rows).T
    table = table[jax.random.permutation(jax.random.fold_in(own, 1), rows)]
    offset_by = jax.random.randint(jax.random.fold_in(own, 2), (rows, 1), 0, top)
    return jnp.take_along_axis(table, (jnp.arange(top)[None, :] + offset_by) % top, axis=1)


def shares(number_of, total, reach, slope, full):
    loads = [(1 << 20) // math.isqrt(grade ** slope) + 1 for grade in range(1, number_of + 1)]
    largest = reach if full else min(reach, max(-(-total // number_of), total * loads[0] // sum(loads)))
    least = 1 if total - largest >= number_of - 1 else 0
    given, rest = [largest] + [least] * (number_of - 1), total - largest - least * (number_of - 1)
    while rest > 0:
        candidates = [i for i in range(1, number_of) if given[i] < largest] or [i for i in range(1, number_of) if given[i] < reach]
        mass, budget = sum([loads[i] for i in candidates]), rest
        for i in candidates:
            extra = min(reach - given[i], max(1, budget * loads[i] // mass), rest)
            given[i] = given[i] + extra
            rest = rest - extra
    return np.array(given)


def scatter_about(key, dims, spread, most, pieces=(), kind=jnp.bfloat16):
    values = spread * jax.random.normal(key, dims, jnp.float32)
    if pieces:
        values = values * levels(key, dims, pieces, -0.22, 0.18)
    return jnp.clip(values, -most, most).astype(kind)


def setup_inputs(seed: int = 0) -> dict:
    keys = jax.random.split(jax.random.key(seed), 11)
    adjoint_start = scatter_about(keys[0], (2, NX, NY), 0.5, 4.0, ((1, 8), (2, 16)), jnp.float32)
    velocity = scatter_about(keys[1], (2, NX, NY), 1.0, 6.0, ((1, 8), (2, 16)), jnp.float32)
    viscosity = jnp.clip(jnp.exp(math.log(1.0) - 2.3025851 * jax.random.uniform(keys[2], (NX, NY), jnp.float32) ** levels(keys[2], (NX, NY), ((0, 8), (1, 16)), -0.2, 0.2)), 0.1, 1.0)
    friction = jnp.clip(jnp.exp(math.log(2.0) - 2.9957323 * jax.random.uniform(keys[3], (NX, NY), jnp.float32) ** levels(keys[3], (NX, NY), ((0, 8), (1, 16)), -0.2, 0.2)), 0.1, 2.0)
    ice_mask = place_ends((jax.random.randint(keys[4], (NX, NY), 0, 8) < 7).astype(jnp.int32), jax.random.fold_in(keys[4], 1), 0, 1)
    misfit = scatter_about(keys[5], (ROWS, BLOCK), 1.0, 6.0, ((0, 128),), jnp.float32)
    heading = jnp.clip(jax.random.uniform(keys[6], (ROWS,), jnp.float32, -3.140625, 3.140625), -3.140625, 3.140625)
    row_dest_keys = jax.random.split(jax.random.fold_in(keys[7], 1), ROWS // ROWS_DEV)
    row_dest_turns = jax.random.permutation(jax.random.fold_in(keys[7], 3), ROWS // ROWS_DEV)
    row_dest = jax.vmap(lambda own, number: shared_out(jax.random.fold_in(keys[7], 2), own, number, ROWS_DEV, TILES, 1, SLOTS, 2))(row_dest_keys, row_dest_turns).reshape((ROWS, 1))
    live_rows = draw_live_rows(jax.random.fold_in(keys[10], 71), 0)
    pixel_lists = draw_pixel_lists(jax.random.fold_in(keys[10], 71), 0)
    return dict(adjoint_start=adjoint_start, velocity=velocity, viscosity=viscosity, friction=friction, ice_mask=ice_mask, misfit=misfit, heading=heading, row_dest=row_dest, live_rows=live_rows, pixel_lists=pixel_lists)


tau_step = 0.04


def diff_rows(field):
    return field[..., 1:, :] - field[..., :-1, :]


def diff_cols(field):
    return field[..., :, 1:] - field[..., :, :-1]


def back_rows(flux):
    return flux[..., :-1, :] - flux[..., 1:, :]


def back_cols(flux):
    return flux[..., :, :-1] - flux[..., :, 1:]


def centre_rows(field):
    return 0.5 * (field[..., 2:, :] - field[..., :-2, :])


def centre_cols(field):
    return 0.5 * (field[..., :, 2:] - field[..., :, :-2])


def operate(padded, eta_pad, fric):
    east = padded[0]
    north = padded[1]
    face_rows = 0.5 * (eta_pad[1:, :] + eta_pad[:-1, :])
    face_cols = 0.5 * (eta_pad[:, 1:] + eta_pad[:, :-1])

    def along_rows(field):
        return back_rows(face_rows * diff_rows(field))[:, 1:-1]

    def along_cols(field):
        return back_cols(face_cols * diff_cols(field))[1:-1, :]

    def mixed_rc(field):
        return centre_rows(eta_pad[:, 1:-1] * centre_cols(field))

    def mixed_cr(field):
        return centre_cols(eta_pad[1:-1, :] * centre_rows(field))

    out_east = 4.0 * along_rows(east) + along_cols(east) - 2.0 * mixed_rc(north) - mixed_cr(north) + fric * east[1:-1, 1:-1]
    out_north = along_rows(north) + 4.0 * along_cols(north) - 2.0 * mixed_cr(east) - mixed_rc(east) + fric * north[1:-1, 1:-1]
    return jnp.stack([out_east, out_north])


def reference(adjoint_start, velocity, viscosity, friction, ice_mask, misfit, heading, row_dest, live_rows, pixel_lists):
    maskf = ice_mask.astype(jnp.float32)
    dest = row_dest[:, 0].reshape(TILES, ROWS_DEV).astype(jnp.int32)
    onehot = (dest[:, :, None] == jnp.arange(TILES, dtype=jnp.int32)[None, None, :]).astype(jnp.int32)
    slot = jnp.sum((jnp.cumsum(onehot, axis=1) - onehot) * onehot, axis=2).astype(jnp.int32)
    live = (jnp.arange(ROWS_DEV, dtype=jnp.int32)[None, :] < live_rows[:, None]).astype(jnp.float32)
    source = jnp.broadcast_to(jnp.arange(TILES, dtype=jnp.int32)[:, None], (TILES, ROWS_DEV))
    lists = pixel_lists[dest * TILES + source, slot]
    grid_rows = (dest // N_GY)[:, :, None] * TX + lists[:, :, 0, :]
    grid_cols = (dest % N_GY)[:, :, None] * TY + lists[:, :, 1, :]
    amount = live[:, :, None] * misfit.reshape(TILES, ROWS_DEV, BLOCK)
    angle = heading.reshape(TILES, ROWS_DEV)[:, :, None]
    load_east = jnp.zeros((NX, NY), jnp.float32).at[grid_rows, grid_cols].add(amount * jnp.cos(angle))
    load_north = jnp.zeros((NX, NY), jnp.float32).at[grid_rows, grid_cols].add(amount * jnp.sin(angle))
    load = jnp.stack([load_east, load_north]) * maskf
    eta_pad = jnp.pad(viscosity, 1)
    adjoint = adjoint_start
    for sweep in range(ITERS):
        masked = maskf * adjoint
        padded = jnp.pad(masked, ((0, 0), (1, 1), (1, 1)))
        image = maskf * operate(padded, eta_pad, friction) + (1.0 - maskf) * adjoint
        adjoint = adjoint + tau_step * (load - image)
    gradient = -maskf * friction * (velocity[0] * adjoint[0] + velocity[1] * adjoint[1])
    return adjoint, gradient
```

```python
import functools

import jax
import jax.numpy as jnp
from jax import lax
from jax.experimental import pallas as pl
from jax.experimental.pallas import tpu as pltpu
from jax.sharding import PartitionSpec as P

ITERS = 4
TAU = 0.04
MESH = pl.DeviceIdType.MESH
F32 = jnp.float32
BF16 = jnp.bfloat16
NT = (((1,), (1,)), ((), ()))
NN = (((1,), (0,)), ((), ()))


def mm(a, b, dims=NN):
    return lax.dot_general(a, b, dims, preferred_element_type=F32)


def halves(x):
    high = x.astype(BF16)
    return high, (x - high.astype(F32)).astype(BF16)


def hot(ids, count, sub):
    base = lax.broadcasted_iota(jnp.int32, (count, ids.shape[1]), 0).astype(F32).astype(BF16)
    return [base[i : i + sub] == ids for i in range(0, count, sub)]


def route(live_ref, dest_ref, heading_ref, misfit_ref, out_ref):
    tiles = out_ref.shape[0]
    own = misfit_ref.shape[0]
    dest = dest_ref[...]
    row_id = lax.broadcasted_iota(jnp.int32, (1, own), 1)
    live = row_id < live_ref[0]
    one = lax.broadcasted_iota(jnp.int32, (tiles, own), 0) == dest
    onehot = jnp.where(one, 1.0, 0.0)
    earlier = jnp.where(
        lax.broadcasted_iota(jnp.int32, (own, own), 0) < lax.broadcasted_iota(jnp.int32, (own, own), 1),
        1.0,
        0.0,
    ).astype(BF16)
    before = mm(onehot.astype(BF16), earlier)
    slot = jnp.sum(before * onehot, axis=0, keepdims=True).astype(jnp.int32)
    position = jnp.where(live, dest * 8 + slot, -1)
    angle = heading_ref[...]
    v_high, v_low = halves(misfit_ref[...])
    step = 256
    for first in range(0, tiles * 8, step):
        here = lax.broadcasted_iota(jnp.int32, (step, own), 0) + first == position
        for comp, factor in enumerate((jnp.cos(angle), jnp.sin(angle))):
            f_high, f_low = halves(factor)
            s_high = jnp.where(here, f_high.astype(F32), 0.0).astype(BF16)
            s_low = jnp.where(here, f_low.astype(F32), 0.0).astype(BF16)
            part = mm(s_high, v_high) + (mm(s_high, v_low) + mm(s_low, v_high))
            out_ref[first // 8 : (first + step) // 8, 8 * comp : 8 * comp + 8, :] = part.reshape(step // 8, 8, 128)


def scatter_group(rows8, cols8, values, acc_ref):
    left, right = [], []
    sub = 16
    zero = jnp.zeros((sub, 128), BF16)
    unit = jnp.ones((sub, 128), BF16)
    for rows, cols, pair in zip(rows8, cols8, values):
        for k in range(8):
            r = jnp.broadcast_to(rows[k : k + 1].astype(F32), (sub, 128)).astype(BF16)
            c = jnp.broadcast_to(cols[k : k + 1].astype(F32), (sub, 128)).astype(BF16)
            pieces = []
            for v in pair:
                pieces += halves(jnp.broadcast_to(v[k : k + 1], (sub, 128)))
            at_row = hot(r, 128, sub)
            left.append(jnp.concatenate([jnp.where(m, p, zero) for p in pieces for m in at_row], axis=0))
            right.append(jnp.concatenate([jnp.where(m, unit, zero) for m in hot(c, 256, sub)], axis=0))
    acc_ref[...] += mm(jnp.concatenate(left, axis=1), jnp.concatenate(right, axis=1), NT)


def scatter(lists_ref, values_ref, load_ref, acc):
    tiles = values_ref.shape[0]
    group = 8
    acc[...] = jnp.zeros_like(acc)

    def step(t, carry):
        sources = [t * group + q for q in range(group)]
        scatter_group(
            [lists_ref[s, :, 0, :] for s in sources],
            [lists_ref[s, :, 1, :] for s in sources],
            [(values_ref[s, 0:8, :], values_ref[s, 8:16, :]) for s in sources],
            acc,
        )
        return carry

    lax.fori_loop(0, tiles // group, step, 0)
    load_ref[0] = acc[0:128] + acc[128:256]
    load_ref[1] = acc[256:384] + acc[384:512]


def neighbours(gx, gy, n_gx, n_gy):
    found = []
    for dx in (-1, 0, 1):
        for dy in (-1, 0, 1):
            if dx or dy:
                found.append((dx, dy, lax.rem(gx + dx + n_gx, n_gx), lax.rem(gy + dy + n_gy, n_gy)))
    return found


def pack_rows(field):
    first = lax.broadcasted_iota(jnp.int32, (8, 256), 0) < 4
    return jnp.where(first, field[0:8], field[120:128])


def pack_cols(field):
    first = lax.broadcasted_iota(jnp.int32, (128, 128), 1) < 64
    return jnp.where(first, field[:, 0:128], field[:, 128:256])


def up(f):
    return pltpu.roll(f, f.shape[0] - 1, 0)


def down(f):
    return pltpu.roll(f, 1, 0)


def right(f):
    return pltpu.roll(f, f.shape[1] - 1, 1)


def left(f):
    return pltpu.roll(f, 1, 1)


def apply(e, n, eta, cx, cy, fric):
    e_up, e_right = up(e), right(e)
    n_up, n_right = up(n), right(n)
    ge = 0.5 * eta * (e_up - down(e))
    he = 0.5 * eta * (e_right - left(e))
    gn = 0.5 * eta * (n_up - down(n))
    hn = 0.5 * eta * (n_right - left(n))
    pe, qe = 4.0 * cx * (e_up - e), cy * (e_right - e)
    pn, qn = cx * (n_up - n), 4.0 * cy * (n_right - n)
    gn, he = 0.5 * gn, 0.5 * he
    out_e = down(pe + hn) - pe - up(hn) + left(qe + gn) - qe - right(gn) + fric * e
    out_n = down(pn + he) - pn - up(he) + left(qn + ge) - qn - right(ge) + fric * n
    return out_e, out_n


def stencil(
    n_gx,
    n_gy,
    load_ref,
    start_ref,
    visc_ref,
    fric_ref,
    mask_ref,
    vel_ref,
    adj_ref,
    grad_ref,
    ext,
    send_rows,
    send_cols,
    got_rows,
    got_cols,
    got_corners,
    send_sem,
    recv_sem,
):
    gx, gy = lax.axis_index("gx"), lax.axis_index("gy")
    around = neighbours(gx, gy, n_gx, n_gy)
    barrier = pltpu.get_barrier_semaphore()
    for _, _, x, y in around:
        pl.semaphore_signal(barrier, inc=1, device_id=(x, y), device_id_type=MESH)
    fields = [load_ref[0], load_ref[1], start_ref[0], start_ref[1], visc_ref[...], fric_ref[...], mask_ref[...].astype(F32)]
    for i, f in enumerate(fields):
        ext[i, 0:128, 0:256] = f
        send_rows[i] = pack_rows(f)
        send_cols[i] = pack_cols(f)
        send_corner = jnp.where(
            lax.broadcasted_iota(jnp.int32, (8, 128), 0) < 4, send_cols[i, 0:8], send_cols[i, 120:128]
        )
        send_cols[i + len(fields), 0:8] = send_corner
    pl.semaphore_wait(barrier, 8)
    copies = []
    for slot, (dx, dy, x, y) in enumerate(around):
        if dy == 0:
            src, dst = send_rows, got_rows.at[(dx + 1) // 2]
        elif dx == 0:
            src, dst = send_cols.at[0:7], got_cols.at[(dy + 1) // 2]
        else:
            src, dst = send_cols.at[7:14, 0:8], got_corners.at[(dx + 1) + (dy + 1) // 2]
        copy = pltpu.make_async_remote_copy(
            src_ref=src,
            dst_ref=dst,
            send_sem=send_sem.at[slot],
            recv_sem=recv_sem.at[slot],
            device_id=(x, y),
            device_id_type=MESH,
        )
        copy.start()
        copies.append(copy)
    for copy in copies:
        copy.wait()
    has = lambda ok, value: jnp.where(ok, value, 0.0)
    top, bottom, west, east = gx > 0, gx < n_gx - 1, gy > 0, gy < n_gy - 1
    both = jnp.logical_and
    for i in range(7):
        sub = lax.broadcasted_iota(jnp.int32, (8, 256), 0) < 4
        ext[i, 128:136, 0:256] = jnp.where(sub, has(bottom, got_rows[0, i]), has(top, got_rows[1, i]))
        lane = lax.broadcasted_iota(jnp.int32, (128, 128), 1)
        value = jnp.where(lane < 64, has(east, got_cols[0, i]), has(west, got_cols[1, i]))
        ext[i, 0:128, 256:384] = jnp.where((lane < 4) | (lane >= 124), value, 0.0)
        lane = lax.broadcasted_iota(jnp.int32, (8, 128), 1)
        sub = lax.broadcasted_iota(jnp.int32, (8, 128), 0) < 4
        below = jnp.where(lane < 64, has(both(bottom, east), got_corners[0, i]), has(both(bottom, west), got_corners[1, i]))
        above = jnp.where(lane < 64, has(both(top, east), got_corners[2, i]), has(both(top, west), got_corners[3, i]))
        value = jnp.where(sub, below, above)
        ext[i, 128:136, 256:384] = jnp.where((lane < 4) | (lane >= 124), value, 0.0)
    eta, fric, mask = ext[4], ext[5], ext[6]
    cx, cy = 0.5 * (eta + up(eta)), 0.5 * (eta + right(eta))
    ext[7], ext[8] = cx, cy
    weight = TAU * mask
    ext[9] = weight
    ext[0] = weight * ext[0]
    ext[1] = weight * ext[1]
    ext[2] = mask * ext[2]
    ext[3] = mask * ext[3]

    def sweep(_, carry):
        out_e, out_n = apply(ext[2], ext[3], ext[4], ext[7], ext[8], ext[5])
        ext[2] = ext[2] + (ext[0] - ext[9] * out_e)
        ext[3] = ext[3] + (ext[1] - ext[9] * out_n)
        return carry

    lax.fori_loop(0, ITERS, sweep, 0)
    on_ice = mask_ref[...] > 0
    keep = (1.0 - TAU) ** ITERS
    w_e, w_n = ext[2, 0:128, 0:256], ext[3, 0:128, 0:256]
    adj_ref[0] = jnp.where(on_ice, w_e, keep * start_ref[0])
    adj_ref[1] = jnp.where(on_ice, w_n, keep * start_ref[1])
    grad_ref[...] = -(fric_ref[...] * (vel_ref[0] * w_e + vel_ref[1] * w_n))


VMEM = pl.BlockSpec(memory_space=pltpu.VMEM)
SMEM = pl.BlockSpec(memory_space=pltpu.SMEM)


def shards(n_gx, n_gy, start, velocity, viscosity, friction, ice_mask, misfit, heading, row_dest, live_rows, lists):
    tiles = n_gx * n_gy
    own = misfit.shape[0]
    outgoing = pl.pallas_call(
        route,
        out_shape=jax.ShapeDtypeStruct((tiles, 16, 128), F32),
        in_specs=[SMEM, VMEM, VMEM, VMEM],
        out_specs=VMEM,
        compiler_params=pltpu.CompilerParams(vmem_limit_bytes=32 << 20),
        name="route",
    )(live_rows, row_dest.reshape(1, own), heading.reshape(1, own), misfit)
    arrived = lax.all_to_all(outgoing, ("gx", "gy"), split_axis=0, concat_axis=0, tiled=True)
    load = pl.pallas_call(
        scatter,
        out_shape=jax.ShapeDtypeStruct((2, 128, 256), F32),
        in_specs=[VMEM] * 2,
        out_specs=VMEM,
        scratch_shapes=[pltpu.VMEM((512, 256), F32)],
        compiler_params=pltpu.CompilerParams(vmem_limit_bytes=40 << 20),
        name="scatter",
    )(lists, arrived)
    return pl.pallas_call(
        functools.partial(stencil, n_gx, n_gy),
        out_shape=(jax.ShapeDtypeStruct((2, 128, 256), F32), jax.ShapeDtypeStruct((128, 256), F32)),
        in_specs=[VMEM] * 6,
        out_specs=(VMEM, VMEM),
        scratch_shapes=[
            pltpu.VMEM((10, 136, 384), F32),
            pltpu.VMEM((7, 8, 256), F32),
            pltpu.VMEM((14, 128, 128), F32),
            pltpu.VMEM((2, 7, 8, 256), F32),
            pltpu.VMEM((2, 7, 128, 128), F32),
            pltpu.VMEM((4, 7, 8, 128), F32),
            pltpu.SemaphoreType.DMA((8,)),
            pltpu.SemaphoreType.DMA((8,)),
        ],
        compiler_params=pltpu.CompilerParams(collective_id=0, has_side_effects=True, vmem_limit_bytes=40 << 20),
        name="stencil",
    )(load, start, viscosity, friction, ice_mask, velocity)


def solution(mesh):
    in_specs = (
        P(None, "gx", "gy"),
        P(None, "gx", "gy"),
        P("gx", "gy"),
        P("gx", "gy"),
        P("gx", "gy"),
        P(("gx", "gy"), None),
        P(("gx", "gy")),
        P(("gx", "gy"), None),
        P(("gx", "gy")),
        P(("gx", "gy"), None, None, None),
    )
    return jax.shard_map(
        functools.partial(shards, mesh.shape["gx"], mesh.shape["gy"]),
        mesh=mesh,
        in_specs=in_specs,
        out_specs=(P(None, "gx", "gy"), P("gx", "gy")),
        check_vma=False,
    )
```

```python
import functools

import jax
import jax.numpy as jnp
from jax import lax
from jax.experimental import pallas as pl
from jax.experimental.pallas import tpu as pltpu
from jax.sharding import PartitionSpec as P

ITERS = 4
TAU = 0.04
MESH = pl.DeviceIdType.MESH
F32 = jnp.float32
BF16 = jnp.bfloat16
NT = (((1,), (1,)), ((), ()))
NN = (((1,), (0,)), ((), ()))


def mm(a, b, dims=NN):
    return lax.dot_general(a, b, dims, preferred_element_type=F32)


def halves(x):
    high = x.astype(BF16)
    return high, (x - high.astype(F32)).astype(BF16)


def hot(ids, count, sub):
    base = lax.broadcasted_iota(jnp.int32, (count, ids.shape[1]), 0).astype(F32).astype(BF16)
    return [base[i : i + sub] == ids for i in range(0, count, sub)]


def route(live_ref, dest_ref, heading_ref, misfit_ref, out_ref):
    tiles = out_ref.shape[0]
    own = misfit_ref.shape[0]
    dest = dest_ref[...]
    row_id = lax.broadcasted_iota(jnp.int32, (1, own), 1)
    live = row_id < live_ref[0]
    one = lax.broadcasted_iota(jnp.int32, (tiles, own), 0) == dest
    onehot = jnp.where(one, 1.0, 0.0)
    earlier = jnp.where(
        lax.broadcasted_iota(jnp.int32, (own, own), 0) < lax.broadcasted_iota(jnp.int32, (own, own), 1),
        1.0,
        0.0,
    ).astype(BF16)
    before = mm(onehot.astype(BF16), earlier)
    slot = jnp.sum(before * onehot, axis=0, keepdims=True).astype(jnp.int32)
    position = jnp.where(live, dest * 8 + slot, -1)
    angle = heading_ref[...]
    v_high, v_low = halves(misfit_ref[...])
    step = 256
    for first in range(0, tiles * 8, step):
        here = lax.broadcasted_iota(jnp.int32, (step, own), 0) + first == position
        for comp, factor in enumerate((jnp.cos(angle), jnp.sin(angle))):
            f_high, f_low = halves(factor)
            s_high = jnp.where(here, f_high.astype(F32), 0.0).astype(BF16)
            s_low = jnp.where(here, f_low.astype(F32), 0.0).astype(BF16)
            part = mm(s_high, v_high) + (mm(s_high, v_low) + mm(s_low, v_high))
            out_ref[first // 8 : (first + step) // 8, 8 * comp : 8 * comp + 8, :] = part.reshape(step // 8, 8, 128)


def scatter_group(rows8, cols8, values, acc_ref):
    left, right = [], []
    sub = 16
    zero = jnp.zeros((sub, 128), BF16)
    unit = jnp.ones((sub, 128), BF16)
    for rows, cols, pair in zip(rows8, cols8, values):
        for k in range(8):
            r = jnp.broadcast_to(rows[k : k + 1].astype(F32), (sub, 128)).astype(BF16)
            c = jnp.broadcast_to(cols[k : k + 1].astype(F32), (sub, 128)).astype(BF16)
            pieces = []
            for v in pair:
                pieces += halves(jnp.broadcast_to(v[k : k + 1], (sub, 128)))
            at_row = hot(r, 128, sub)
            left.append(jnp.concatenate([jnp.where(m, p, zero) for p in pieces for m in at_row], axis=0))
            right.append(jnp.concatenate([jnp.where(m, unit, zero) for m in hot(c, 256, sub)], axis=0))
    acc_ref[...] += mm(jnp.concatenate(left, axis=1), jnp.concatenate(right, axis=1), NT)


def neighbours(gx, gy, n_gx, n_gy):
    found = []
    for dx in (-1, 0, 1):
        for dy in (-1, 0, 1):
            if dx or dy:
                found.append((dx, dy, lax.rem(gx + dx + n_gx, n_gx), lax.rem(gy + dy + n_gy, n_gy)))
    return found


def pack_rows(field):
    first = lax.broadcasted_iota(jnp.int32, (8, 256), 0) < 4
    return jnp.where(first, field[0:8], field[120:128])


def pack_cols(field):
    first = lax.broadcasted_iota(jnp.int32, (128, 128), 1) < 64
    return jnp.where(first, field[:, 0:128], field[:, 128:256])


def up(f):
    return pltpu.roll(f, f.shape[0] - 1, 0)


def down(f):
    return pltpu.roll(f, 1, 0)


def right(f):
    return pltpu.roll(f, f.shape[1] - 1, 1)


def left(f):
    return pltpu.roll(f, 1, 1)


def apply(e, n, eta, cx, cy, fric):
    e_up, e_right = up(e), right(e)
    n_up, n_right = up(n), right(n)
    ge = 0.5 * eta * (e_up - down(e))
    he = 0.5 * eta * (e_right - left(e))
    gn = 0.5 * eta * (n_up - down(n))
    hn = 0.5 * eta * (n_right - left(n))
    pe, qe = 4.0 * cx * (e_up - e), cy * (e_right - e)
    pn, qn = cx * (n_up - n), 4.0 * cy * (n_right - n)
    gn, he = 0.5 * gn, 0.5 * he
    out_e = down(pe + hn) - pe - up(hn) + left(qe + gn) - qe - right(gn) + fric * e
    out_n = down(pn + he) - pn - up(he) + left(qn + ge) - qn - right(ge) + fric * n
    return out_e, out_n


def fill_edges(ext, fields, flags, rows, cols, corners):
    top, bottom, west, east = flags
    has = lambda ok, value: jnp.where(ok, value, 0.0)
    both = jnp.logical_and
    for i, field in enumerate(fields):
        sub = lax.broadcasted_iota(jnp.int32, (8, 256), 0) < 4
        ext[field, 128:136, 0:256] = jnp.where(sub, has(bottom, rows[0, i]), has(top, rows[1, i]))
        lane = lax.broadcasted_iota(jnp.int32, (128, 128), 1)
        value = jnp.where(lane < 64, has(east, cols[0, i]), has(west, cols[1, i]))
        ext[field, 0:128, 256:384] = jnp.where((lane < 4) | (lane >= 124), value, 0.0)
        lane = lax.broadcasted_iota(jnp.int32, (8, 128), 1)
        sub = lax.broadcasted_iota(jnp.int32, (8, 128), 0) < 4
        below = jnp.where(lane < 64, has(both(bottom, east), corners[0, i]), has(both(bottom, west), corners[1, i]))
        above = jnp.where(lane < 64, has(both(top, east), corners[2, i]), has(both(top, west), corners[3, i]))
        value = jnp.where(sub, below, above)
        ext[field, 128:136, 256:384] = jnp.where((lane < 4) | (lane >= 124), value, 0.0)


def edge_copies(around, packed, got, sems):
    rows, cols, corner = packed
    got_rows, got_cols, got_corners = got
    copies = []
    for slot, (dx, dy, x, y) in enumerate(around):
        if dy == 0:
            src, dst = rows, got_rows.at[(dx + 1) // 2]
        elif dx == 0:
            src, dst = cols, got_cols.at[(dy + 1) // 2]
        else:
            src, dst = corner, got_corners.at[(dx + 1) + (dy + 1) // 2]
        copies.append(
            pltpu.make_async_remote_copy(
                src_ref=src,
                dst_ref=dst,
                send_sem=sems.at[0, slot],
                recv_sem=sems.at[1, slot],
                device_id=(x, y),
                device_id_type=MESH,
            )
        )
    return copies


def pack_edge(i, field, packed):
    rows, cols, corner = packed
    rows[i] = pack_rows(field)
    cols[i] = pack_cols(field)
    first = lax.broadcasted_iota(jnp.int32, (8, 128), 0) < 4
    corner[i] = jnp.where(first, cols[i, 0:8], cols[i, 120:128])


def body(
    n_gx,
    n_gy,
    live_ref,
    dest_hbm,
    heading_hbm,
    misfit_hbm,
    start_hbm,
    visc_hbm,
    fric_hbm,
    mask_hbm,
    vel_hbm,
    lists_hbm,
    adj_ref,
    grad_ref,
    dest_ref,
    heading_ref,
    misfit_ref,
    start_ref,
    visc_ref,
    fric_ref,
    mask_ref,
    vel_ref,
    lists,
    outgoing,
    arrived,
    acc,
    ext,
    fixed_rows,
    fixed_cols,
    fixed_corner,
    fixed_got_rows,
    fixed_got_cols,
    fixed_got_corners,
    load_rows,
    load_cols,
    load_corner,
    load_got_rows,
    load_got_cols,
    load_got_corners,
    in_sems,
    send_sem,
    recv_sem,
    fixed_sems,
    load_sems,
    all_sem,
):
    gx, gy = lax.axis_index("gx"), lax.axis_index("gy")
    me = gx * n_gy + gy
    around = neighbours(gx, gy, n_gx, n_gy)
    loads = [
        pltpu.make_async_copy(src, dst, in_sems.at[i])
        for i, (src, dst) in enumerate(
            [
                (dest_hbm, dest_ref),
                (heading_hbm, heading_ref),
                (misfit_hbm, misfit_ref),
                (start_hbm, start_ref),
                (visc_hbm, visc_ref),
                (fric_hbm, fric_ref),
                (mask_hbm, mask_ref),
                (lists_hbm, lists),
                (vel_hbm, vel_ref),
            ]
        )
    ]
    for copy in loads:
        copy.start()

    barrier = pltpu.get_barrier_semaphore()
    for a in range(1, n_gx):
        pl.semaphore_signal(barrier, inc=1, device_id=(lax.rem(gx + a, n_gx), gy), device_id_type=MESH)
    for b in range(1, n_gy):
        pl.semaphore_signal(barrier, inc=1, device_id=(gx, lax.rem(gy + b, n_gy)), device_id_type=MESH)

    for copy in loads[0:3]:
        copy.wait()
    route(live_ref, dest_ref, heading_ref, misfit_ref, outgoing)
    acc[...] = jnp.zeros_like(acc)
    fixed_packed = (fixed_rows, fixed_cols, fixed_corner)
    for copy in loads[3:7]:
        copy.wait()
    fields = [start_ref[0], start_ref[1], visc_ref[...], fric_ref[...], mask_ref[...].astype(F32)]
    for i, f in enumerate(fields):
        ext[2 + i, 0:128, 0:256] = f
        pack_edge(i, f, fixed_packed)

    pl.semaphore_wait(barrier, n_gx + n_gy - 2)
    for b in range(1, n_gy):
        pl.semaphore_signal(all_sem, inc=1, device_id=(gx, lax.rem(gy + b, n_gy)), device_id_type=MESH)
    pl.semaphore_wait(all_sem, n_gy - 1)

    fixed_got = (fixed_got_rows, fixed_got_cols, fixed_got_corners)
    fixed_copies = edge_copies(around, fixed_packed, fixed_got, fixed_sems)
    for copy in fixed_copies:
        copy.start()

    def send_group(g, first=0):
        y = lax.rem(gy + g, n_gy)
        for a in range(first, n_gx):
            x = lax.rem(gx + a, n_gx)
            pltpu.make_async_remote_copy(
                src_ref=outgoing.at[x * n_gy + y],
                dst_ref=arrived.at[gy, gx],
                send_sem=send_sem,
                recv_sem=recv_sem.at[g],
                device_id=(x, y),
                device_id_type=MESH,
            ).start()

    pltpu.make_async_copy(outgoing.at[me], arrived.at[gy, gx], recv_sem.at[0]).start()
    send_group(0, 1)
    send_group(1)

    for copy in fixed_copies:
        copy.wait_recv()
    flags = (gx > 0, gx < n_gx - 1, gy > 0, gy < n_gy - 1)
    fill_edges(ext, range(2, 7), flags, *fixed_got)
    eta, fric, mask = ext[4], ext[5], ext[6]
    ext[7], ext[8] = 0.5 * (eta + up(eta)), 0.5 * (eta + right(eta))
    ext[9] = TAU * mask
    ext[2] = mask * ext[2]
    ext[3] = mask * ext[3]
    out_e, out_n = apply(ext[2], ext[3], ext[4], ext[7], ext[8], ext[5])
    ext[2] = ext[2] - ext[9] * out_e
    ext[3] = ext[3] - ext[9] * out_n
    for copy in loads[7:9]:
        copy.wait()

    def take_group(g):
        y = lax.rem(gy + n_gy - g, n_gy)
        pltpu.make_async_copy(outgoing.at[0:n_gx], arrived.at[y], recv_sem.at[g]).wait()
        sources = [x * n_gy + y for x in range(n_gx)]
        scatter_group(
            [lists[s, :, 0, :] for s in sources],
            [lists[s, :, 1, :] for s in sources],
            [(arrived[y, x, 0:8, :], arrived[y, x, 8:16, :]) for x in range(n_gx)],
            acc,
        )

    def send_and_take(g, carry):
        send_group(g + 2)
        take_group(g)
        return carry

    def take(g, carry):
        take_group(g)
        return carry

    lax.fori_loop(0, n_gy - 2, send_and_take, 0)
    lax.fori_loop(n_gy - 2, n_gy, take, 0)

    load_packed = (load_rows, load_cols, load_corner)
    for i in range(2):
        f = acc[256 * i : 256 * i + 128] + acc[256 * i + 128 : 256 * i + 256]
        ext[i, 0:128, 0:256] = f
        pack_edge(i, f, load_packed)
    load_got = (load_got_rows, load_got_cols, load_got_corners)
    load_copies = edge_copies(around, load_packed, load_got, load_sems)
    for copy in load_copies:
        copy.start()
    for copy in load_copies:
        copy.wait_recv()
    fill_edges(ext, range(2), flags, *load_got)
    ext[0] = ext[9] * ext[0]
    ext[1] = ext[9] * ext[1]
    ext[2] = ext[2] + ext[0]
    ext[3] = ext[3] + ext[1]

    def sweep(_, carry):
        out_e, out_n = apply(ext[2], ext[3], ext[4], ext[7], ext[8], ext[5])
        ext[2] = ext[2] + (ext[0] - ext[9] * out_e)
        ext[3] = ext[3] + (ext[1] - ext[9] * out_n)
        return carry

    lax.fori_loop(0, ITERS - 1, sweep, 0)
    on_ice = mask_ref[...] > 0
    keep = (1.0 - TAU) ** ITERS
    w_e, w_n = ext[2, 0:128, 0:256], ext[3, 0:128, 0:256]
    adj_ref[0] = jnp.where(on_ice, w_e, keep * start_ref[0])
    adj_ref[1] = jnp.where(on_ice, w_n, keep * start_ref[1])
    grad_ref[...] = -(fric_ref[...] * (vel_ref[0] * w_e + vel_ref[1] * w_n))

    for copy in fixed_copies + load_copies:
        copy.wait_send()
    sent = n_gx * n_gy - 1
    pltpu.make_async_remote_copy(
        src_ref=outgoing.at[0:sent],
        dst_ref=outgoing.at[0:sent],
        send_sem=send_sem,
        recv_sem=recv_sem.at[0],
        device_id=(gx, gy),
        device_id_type=MESH,
    ).wait_send()


VMEM = pl.BlockSpec(memory_space=pltpu.VMEM)
SMEM = pl.BlockSpec(memory_space=pltpu.SMEM)
HBM = pl.BlockSpec(memory_space=pltpu.HBM)


def edge_scratch(fields):
    return [
        pltpu.VMEM((fields, 8, 256), F32),
        pltpu.VMEM((fields, 128, 128), F32),
        pltpu.VMEM((fields, 8, 128), F32),
        pltpu.VMEM((2, fields, 8, 256), F32),
        pltpu.VMEM((2, fields, 128, 128), F32),
        pltpu.VMEM((4, fields, 8, 128), F32),
    ]


def shards(n_gx, n_gy, start, velocity, viscosity, friction, ice_mask, misfit, heading, row_dest, live_rows, lists):
    tiles = n_gx * n_gy
    own = misfit.shape[0]
    return pl.pallas_call(
        functools.partial(body, n_gx, n_gy),
        out_shape=(jax.ShapeDtypeStruct((2, 128, 256), F32), jax.ShapeDtypeStruct((128, 256), F32)),
        in_specs=[SMEM] + [HBM] * 9,
        out_specs=(VMEM, VMEM),
        scratch_shapes=[
            pltpu.VMEM((1, own), jnp.int32),
            pltpu.VMEM((1, own), F32),
            pltpu.VMEM(misfit.shape, F32),
            pltpu.VMEM(start.shape, F32),
            pltpu.VMEM(viscosity.shape, F32),
            pltpu.VMEM(friction.shape, F32),
            pltpu.VMEM(ice_mask.shape, jnp.int32),
            pltpu.VMEM(velocity.shape, F32),
            pltpu.VMEM(lists.shape, jnp.int32),
            pltpu.VMEM((tiles, 16, 128), F32),
            pltpu.VMEM((n_gy, n_gx, 16, 128), F32),
            pltpu.VMEM((512, 256), F32),
            pltpu.VMEM((10, 136, 384), F32),
            *edge_scratch(5),
            *edge_scratch(2),
            pltpu.SemaphoreType.DMA((9,)),
            pltpu.SemaphoreType.DMA,
            pltpu.SemaphoreType.DMA((n_gy,)),
            pltpu.SemaphoreType.DMA((2, 8)),
            pltpu.SemaphoreType.DMA((2, 8)),
            pltpu.SemaphoreType.REGULAR,
        ],
        compiler_params=pltpu.CompilerParams(collective_id=0, has_side_effects=True, vmem_limit_bytes=60 << 20),
        name="shelf",
    )(
        live_rows,
        row_dest.reshape(1, own),
        heading.reshape(1, own),
        misfit,
        start,
        viscosity,
        friction,
        ice_mask,
        velocity,
        lists,
    )


def solution(mesh):
    in_specs = (
        P(None, "gx", "gy"),
        P(None, "gx", "gy"),
        P("gx", "gy"),
        P("gx", "gy"),
        P("gx", "gy"),
        P(("gx", "gy"), None),
        P(("gx", "gy")),
        P(("gx", "gy"), None),
        P(("gx", "gy")),
        P(("gx", "gy"), None, None, None),
    )
    return jax.shard_map(
        functools.partial(shards, mesh.shape["gx"], mesh.shape["gy"]),
        mesh=mesh,
        in_specs=in_specs,
        out_specs=(P(None, "gx", "gy"), P("gx", "gy")),
        check_vma=False,
    )
```

```python
import functools

import jax
import jax.numpy as jnp
from jax import lax
from jax.experimental import pallas as pl
from jax.experimental.pallas import tpu as pltpu
from jax.sharding import PartitionSpec as P

ITERS = 4
TAU = 0.04
AHEAD = 6
MESH = pl.DeviceIdType.MESH
F32 = jnp.float32
BF16 = jnp.bfloat16
F8 = jnp.float8_e4m3fn
PIECES = 3
NT = (((1,), (1,)), ((), ()))
NN = (((1,), (0,)), ((), ()))


def mm(a, b, dims=NN):
    return lax.dot_general(a, b, dims, preferred_element_type=F32)


def halves(x):
    high = x.astype(BF16)
    return high, (x - high.astype(F32)).astype(BF16)


def hot(ids, count, sub):
    base = lax.broadcasted_iota(jnp.int32, (count, ids.shape[1]), 0).astype(F32).astype(BF16)
    return [base[i : i + sub] == ids for i in range(0, count, sub)]


def route(live_ref, dest_ref, heading_ref, misfit_ref, out_ref):
    tiles = out_ref.shape[0]
    own = misfit_ref.shape[0]
    dest = dest_ref[...]
    row_id = lax.broadcasted_iota(jnp.int32, (1, own), 1)
    live = row_id < live_ref[0]
    one = lax.broadcasted_iota(jnp.int32, (tiles, own), 0) == dest
    onehot = jnp.where(one, 1.0, 0.0)
    earlier = jnp.where(
        lax.broadcasted_iota(jnp.int32, (own, own), 0) < lax.broadcasted_iota(jnp.int32, (own, own), 1),
        1.0,
        0.0,
    ).astype(BF16)
    before = mm(onehot.astype(BF16), earlier)
    slot = jnp.sum(before * onehot, axis=0, keepdims=True).astype(jnp.int32)
    position = jnp.where(live, dest * 8 + slot, -1)
    angle = heading_ref[...]
    v_high, v_low = halves(misfit_ref[...])
    step = 256
    for first in range(0, tiles * 8, step):
        here = lax.broadcasted_iota(jnp.int32, (step, own), 0) + first == position
        for comp, factor in enumerate((jnp.cos(angle), jnp.sin(angle))):
            f_high, f_low = halves(factor)
            s_high = jnp.where(here, f_high.astype(F32), 0.0).astype(BF16)
            s_low = jnp.where(here, f_low.astype(F32), 0.0).astype(BF16)
            part = mm(s_high, v_high) + (mm(s_high, v_low) + mm(s_low, v_high))
            out_ref[first // 8 : (first + step) // 8, 8 * comp : 8 * comp + 8, :] = part.reshape(step // 8, 8, 128)


def scatter_group(rows8, cols8, values, acc_ref):
    largest = functools.reduce(jnp.maximum, [jnp.abs(v) for pair in values for v in pair])
    largest = jnp.maximum(jnp.max(largest, keepdims=True), 1e-30)
    scale, back = 384.0 / largest, largest * (1.0 / 384.0)
    left, right = [], []
    sub = 16
    zero = jnp.zeros((sub, 128), BF16)
    unit = jnp.ones((sub, 128), BF16)
    for rows, cols, pair in zip(rows8, cols8, values):
        pieces = []
        for v in pair:
            rest = v * scale
            for _ in range(PIECES):
                piece = rest.astype(BF16).astype(F8).astype(F32)
                pieces.append(piece)
                rest = (rest - piece) * 16.0
        for k in range(8):
            r = jnp.broadcast_to(rows[k : k + 1].astype(F32), (sub, 128)).astype(BF16)
            c = jnp.broadcast_to(cols[k : k + 1].astype(F32), (sub, 128)).astype(BF16)
            at_row = hot(r, 128, sub)
            wide = [jnp.broadcast_to(p[k : k + 1], (sub, 128)).astype(BF16) for p in pieces]
            left.append(jnp.concatenate([jnp.where(m, p, zero) for p in wide for m in at_row], axis=0).astype(F8))
            right.append(jnp.concatenate([jnp.where(m, unit, zero) for m in hot(c, 256, sub)], axis=0).astype(F8))
    acc_ref[...] += mm(jnp.concatenate(left, axis=1), jnp.concatenate(right, axis=1), NT) * back


def neighbours(gx, gy, n_gx, n_gy):
    found = []
    for dx in (-1, 0, 1):
        for dy in (-1, 0, 1):
            if dx or dy:
                found.append((dx, dy, lax.rem(gx + dx + n_gx, n_gx), lax.rem(gy + dy + n_gy, n_gy)))
    return found


def pack_rows(field):
    first = lax.broadcasted_iota(jnp.int32, (8, 256), 0) < 4
    return jnp.where(first, field[0:8], field[120:128])


def pack_cols(field):
    first = lax.broadcasted_iota(jnp.int32, (128, 128), 1) < 64
    return jnp.where(first, field[:, 0:128], field[:, 128:256])


def up(f):
    return pltpu.roll(f, f.shape[0] - 1, 0)


def down(f):
    return pltpu.roll(f, 1, 0)


def right(f):
    return pltpu.roll(f, f.shape[1] - 1, 1)


def left(f):
    return pltpu.roll(f, 1, 1)


def apply(e, n, eta, cx, cy, fric):
    e_up, e_right = up(e), right(e)
    n_up, n_right = up(n), right(n)
    ge = 0.5 * eta * (e_up - down(e))
    he = 0.5 * eta * (e_right - left(e))
    gn = 0.5 * eta * (n_up - down(n))
    hn = 0.5 * eta * (n_right - left(n))
    pe, qe = 4.0 * cx * (e_up - e), cy * (e_right - e)
    pn, qn = cx * (n_up - n), 4.0 * cy * (n_right - n)
    gn, he = 0.5 * gn, 0.5 * he
    out_e = down(pe + hn) - pe - up(hn) + left(qe + gn) - qe - right(gn) + fric * e
    out_n = down(pn + he) - pn - up(he) + left(qn + ge) - qn - right(ge) + fric * n
    return out_e, out_n


def fill_edges(ext, fields, flags, rows, cols, corners):
    top, bottom, west, east = flags
    has = lambda ok, value: jnp.where(ok, value, 0.0)
    both = jnp.logical_and
    for i, field in enumerate(fields):
        sub = lax.broadcasted_iota(jnp.int32, (8, 256), 0) < 4
        ext[field, 128:136, 0:256] = jnp.where(sub, has(bottom, rows[0, i]), has(top, rows[1, i]))
        sub = lax.broadcasted_iota(jnp.int32, (8, 128), 0) < 4
        first = jnp.where(sub, has(east, cols[0, i]), 0.0)
        last = jnp.where(sub, 0.0, has(west, cols[1, i]))
        turned = jnp.concatenate([first, jnp.zeros((112, 128), F32), last], axis=0)
        ext[field, 0:128, 256:384] = turned.T
        lane = lax.broadcasted_iota(jnp.int32, (8, 128), 1)
        sub = lax.broadcasted_iota(jnp.int32, (8, 128), 0) < 4
        below = jnp.where(lane < 64, has(both(bottom, east), corners[0, i]), has(both(bottom, west), corners[1, i]))
        above = jnp.where(lane < 64, has(both(top, east), corners[2, i]), has(both(top, west), corners[3, i]))
        value = jnp.where(sub, below, above)
        ext[field, 128:136, 256:384] = jnp.where((lane < 4) | (lane >= 124), value, 0.0)


def edge_copies(around, packed, got, sems):
    rows, cols, corner = packed
    got_rows, got_cols, got_corners = got
    copies = []
    for slot, (dx, dy, x, y) in enumerate(around):
        if dy == 0:
            src, dst = rows, got_rows.at[(dx + 1) // 2]
        elif dx == 0:
            src, dst = cols, got_cols.at[(dy + 1) // 2]
        else:
            src, dst = corner, got_corners.at[(dx + 1) + (dy + 1) // 2]
        copies.append(
            pltpu.make_async_remote_copy(
                src_ref=src,
                dst_ref=dst,
                send_sem=sems.at[0, slot],
                recv_sem=sems.at[1, slot],
                device_id=(x, y),
                device_id_type=MESH,
            )
        )
    return copies


def pack_edge(i, field, packed):
    rows, cols, corner = packed
    rows[i] = pack_rows(field)
    edge = pack_cols(field)
    turned = edge.T
    first = lax.broadcasted_iota(jnp.int32, (8, 128), 0) < 4
    cols[i] = jnp.where(first, turned[0:8], turned[120:128])
    corner[i] = jnp.where(first, edge[0:8], edge[120:128])


def body(
    n_gx,
    n_gy,
    live_ref,
    dest_hbm,
    heading_hbm,
    misfit_hbm,
    start_hbm,
    visc_hbm,
    fric_hbm,
    mask_hbm,
    lists_hbm,
    ice_ref,
    dest_ref,
    heading_ref,
    misfit_ref,
    start_ref,
    visc_ref,
    fric_ref,
    mask_ref,
    lists,
    outgoing,
    arrived,
    acc,
    ext,
    fixed_rows,
    fixed_cols,
    fixed_corner,
    fixed_got_rows,
    fixed_got_cols,
    fixed_got_corners,
    load_rows,
    load_cols,
    load_corner,
    load_got_rows,
    load_got_cols,
    load_got_corners,
    in_sems,
    send_sem,
    recv_sem,
    fixed_sems,
    load_sems,
    all_sem,
):
    gx, gy = lax.axis_index("gx"), lax.axis_index("gy")
    me = gx * n_gy + gy
    around = neighbours(gx, gy, n_gx, n_gy)
    loads = [
        pltpu.make_async_copy(src, dst, in_sems.at[i])
        for i, (src, dst) in enumerate(
            [
                (dest_hbm, dest_ref),
                (heading_hbm, heading_ref),
                (misfit_hbm, misfit_ref),
                (start_hbm, start_ref),
                (visc_hbm, visc_ref),
                (fric_hbm, fric_ref),
                (mask_hbm, mask_ref),
                (lists_hbm, lists),
            ]
        )
    ]
    for copy in loads:
        copy.start()

    barrier = pltpu.get_barrier_semaphore()
    for a in range(1, n_gx):
        pl.semaphore_signal(barrier, inc=1, device_id=(lax.rem(gx + a, n_gx), gy), device_id_type=MESH)
    for b in range(1, n_gy):
        pl.semaphore_signal(barrier, inc=1, device_id=(gx, lax.rem(gy + b, n_gy)), device_id_type=MESH)

    for copy in loads[0:3]:
        copy.wait()
    route(live_ref, dest_ref, heading_ref, misfit_ref, outgoing)
    acc[...] = jnp.zeros_like(acc)
    fixed_packed = (fixed_rows, fixed_cols, fixed_corner)
    for copy in loads[3:7]:
        copy.wait()
    fields = [start_ref[0], start_ref[1], visc_ref[...], fric_ref[...], mask_ref[...].astype(F32)]
    for i, f in enumerate(fields):
        ext[2 + i, 0:128, 0:256] = f
        pack_edge(i, f, fixed_packed)

    pl.semaphore_wait(barrier, n_gx + n_gy - 2)
    fixed_got = (fixed_got_rows, fixed_got_cols, fixed_got_corners)
    fixed_copies = edge_copies(around, fixed_packed, fixed_got, fixed_sems)

    def send_group(g, first=0):
        y = lax.rem(gy + g, n_gy)
        for a in range(first, n_gx):
            x = lax.rem(gx + a, n_gx)
            pltpu.make_async_remote_copy(
                src_ref=outgoing.at[x * n_gy + y],
                dst_ref=arrived.at[gy, gx],
                send_sem=send_sem,
                recv_sem=recv_sem.at[g],
                device_id=(x, y),
                device_id_type=MESH,
            ).start()

    pltpu.make_async_copy(outgoing.at[me], arrived.at[gy, gx], recv_sem.at[0]).start()
    send_group(0, 1)
    for b in range(1, n_gy):
        pl.semaphore_signal(
            all_sem.at[b], inc=1, device_id=(gx, lax.rem(gy + n_gy - b, n_gy)), device_id_type=MESH
        )

    def send_next(g, carry):
        pl.semaphore_wait(all_sem.at[g], 1)
        send_group(g)
        return carry

    lax.fori_loop(1, AHEAD, send_next, 0)
    for copy in loads[7:8]:
        copy.wait()

    def take_group(g):
        y = lax.rem(gy + n_gy - g, n_gy)
        pltpu.make_async_copy(outgoing.at[0:n_gx], arrived.at[y], recv_sem.at[g]).wait()
        sources = [x * n_gy + y for x in range(n_gx)]
        scatter_group(
            [lists[s, :, 0, :] for s in sources],
            [lists[s, :, 1, :] for s in sources],
            [(arrived[y, x, 0:8, :], arrived[y, x, 8:16, :]) for x in range(n_gx)],
            acc,
        )

    def send_and_take(g, carry):
        send_next(g + AHEAD, carry)
        take_group(g)
        return carry

    def take(g, carry):
        take_group(g)
        return carry

    lax.fori_loop(0, n_gy - AHEAD, send_and_take, 0)
    for copy in fixed_copies:
        copy.start()
    lax.fori_loop(n_gy - AHEAD, n_gy, take, 0)

    load_packed = (load_rows, load_cols, load_corner)
    for i in range(2):
        parts = [acc[128 * (PIECES * i + p) : 128 * (PIECES * i + p + 1)] for p in range(PIECES)]
        f = parts[0] + (parts[1] + parts[2] * (1.0 / 16.0)) * (1.0 / 16.0)
        ext[i, 0:128, 0:256] = f
        pack_edge(i, f, load_packed)
    load_got = (load_got_rows, load_got_cols, load_got_corners)
    load_copies = edge_copies(around, load_packed, load_got, load_sems)
    for copy in load_copies:
        copy.start()

    for copy in fixed_copies:
        copy.wait_recv()
    flags = (gx > 0, gx < n_gx - 1, gy > 0, gy < n_gy - 1)
    fill_edges(ext, range(2, 7), flags, *fixed_got)
    eta, fric, mask = ext[4], ext[5], ext[6]
    ext[7], ext[8] = 0.5 * (eta + up(eta)), 0.5 * (eta + right(eta))
    ext[9] = TAU * mask
    ext[2] = mask * ext[2]
    ext[3] = mask * ext[3]
    out_e, out_n = apply(ext[2], ext[3], ext[4], ext[7], ext[8], ext[5])
    ext[2] = ext[2] - ext[9] * out_e
    ext[3] = ext[3] - ext[9] * out_n

    for copy in load_copies:
        copy.wait_recv()
    fill_edges(ext, range(2), flags, *load_got)
    ext[0] = ext[9] * ext[0]
    ext[1] = ext[9] * ext[1]
    ext[2] = ext[2] + ext[0]
    ext[3] = ext[3] + ext[1]

    def sweep(_, carry):
        out_e, out_n = apply(ext[2], ext[3], ext[4], ext[7], ext[8], ext[5])
        ext[2] = ext[2] + (ext[0] - ext[9] * out_e)
        ext[3] = ext[3] + (ext[1] - ext[9] * out_n)
        return carry

    lax.fori_loop(0, ITERS - 1, sweep, 0)
    ice_ref[...] = ext[2:4, 0:128, 0:256]

    for copy in fixed_copies + load_copies:
        copy.wait_send()
    sent = n_gx * n_gy - 1
    pltpu.make_async_remote_copy(
        src_ref=outgoing.at[0:sent],
        dst_ref=outgoing.at[0:sent],
        send_sem=send_sem,
        recv_sem=recv_sem.at[0],
        device_id=(gx, gy),
        device_id_type=MESH,
    ).wait_send()


def finish(ice_ref, start_ref, fric_ref, mask_ref, vel_ref, adj_ref, grad_ref):
    here = mask_ref[...] > 0
    keep = (1.0 - TAU) ** ITERS
    adj_ref[0] = jnp.where(here, ice_ref[0], keep * start_ref[0])
    adj_ref[1] = jnp.where(here, ice_ref[1], keep * start_ref[1])
    grad_ref[...] = -(fric_ref[...] * (vel_ref[0] * ice_ref[0] + vel_ref[1] * ice_ref[1]))


VMEM = pl.BlockSpec(memory_space=pltpu.VMEM)
SMEM = pl.BlockSpec(memory_space=pltpu.SMEM)
HBM = pl.BlockSpec(memory_space=pltpu.HBM)


def edge_scratch(fields):
    return [
        pltpu.VMEM((fields, 8, 256), F32),
        pltpu.VMEM((fields, 8, 128), F32),
        pltpu.VMEM((fields, 8, 128), F32),
        pltpu.VMEM((2, fields, 8, 256), F32),
        pltpu.VMEM((2, fields, 8, 128), F32),
        pltpu.VMEM((4, fields, 8, 128), F32),
    ]


def shards(n_gx, n_gy, start, velocity, viscosity, friction, ice_mask, misfit, heading, row_dest, live_rows, lists):
    tiles = n_gx * n_gy
    own = misfit.shape[0]
    on_ice = pl.pallas_call(
        functools.partial(body, n_gx, n_gy),
        out_shape=jax.ShapeDtypeStruct((2, 128, 256), F32),
        in_specs=[SMEM] + [HBM] * 8,
        out_specs=VMEM,
        scratch_shapes=[
            pltpu.VMEM((1, own), jnp.int32),
            pltpu.VMEM((1, own), F32),
            pltpu.VMEM(misfit.shape, F32),
            pltpu.VMEM(start.shape, F32),
            pltpu.VMEM(viscosity.shape, F32),
            pltpu.VMEM(friction.shape, F32),
            pltpu.VMEM(ice_mask.shape, jnp.int32),
            pltpu.VMEM(lists.shape, jnp.int32),
            pltpu.VMEM((tiles, 16, 128), F32),
            pltpu.VMEM((n_gy, n_gx, 16, 128), F32),
            pltpu.VMEM((2 * PIECES * 128, 256), F32),
            pltpu.VMEM((10, 136, 384), F32),
            *edge_scratch(5),
            *edge_scratch(2),
            pltpu.SemaphoreType.DMA((8,)),
            pltpu.SemaphoreType.DMA,
            pltpu.SemaphoreType.DMA((n_gy,)),
            pltpu.SemaphoreType.DMA((2, 8)),
            pltpu.SemaphoreType.DMA((2, 8)),
            pltpu.SemaphoreType.REGULAR((n_gy,)),
        ],
        compiler_params=pltpu.CompilerParams(collective_id=0, has_side_effects=True, vmem_limit_bytes=60 << 20),
        name="shelf",
    )(
        live_rows,
        row_dest.reshape(1, own),
        heading.reshape(1, own),
        misfit,
        start,
        viscosity,
        friction,
        ice_mask,
        lists,
    )
    return pl.pallas_call(
        finish,
        out_shape=(jax.ShapeDtypeStruct((2, 128, 256), F32), jax.ShapeDtypeStruct((128, 256), F32)),
        in_specs=[VMEM] * 5,
        out_specs=(VMEM, VMEM),
        name="finish",
    )(on_ice, start, friction, ice_mask, velocity)


def solution(mesh):
    in_specs = (
        P(None, "gx", "gy"),
        P(None, "gx", "gy"),
        P("gx", "gy"),
        P("gx", "gy"),
        P("gx", "gy"),
        P(("gx", "gy"), None),
        P(("gx", "gy")),
        P(("gx", "gy"), None),
        P(("gx", "gy")),
        P(("gx", "gy"), None, None, None),
    )
    return jax.shard_map(
        functools.partial(shards, mesh.shape["gx"], mesh.shape["gy"]),
        mesh=mesh,
        in_specs=in_specs,
        out_specs=(P(None, "gx", "gy"), P("gx", "gy")),
        check_vma=False,
    )
```

```python
import functools

import jax
import jax.numpy as jnp
from jax import lax
from jax.experimental import pallas as pl
from jax.experimental.pallas import tpu as pltpu
from jax.sharding import PartitionSpec as P

ITERS = 4
TAU = 0.04
AHEAD = 6
MESH = pl.DeviceIdType.MESH
F32 = jnp.float32
BF16 = jnp.bfloat16
F8 = jnp.float8_e4m3fn
PIECES = 3
NT = (((1,), (1,)), ((), ()))
NN = (((1,), (0,)), ((), ()))


def mm(a, b, dims=NN):
    return lax.dot_general(a, b, dims, preferred_element_type=F32)


def halves(x):
    high = x.astype(BF16)
    return high, (x - high.astype(F32)).astype(BF16)


def hot(ids, count, sub):
    base = lax.broadcasted_iota(jnp.int32, (count, ids.shape[1]), 0).astype(F32).astype(BF16)
    return [base[i : i + sub] == ids for i in range(0, count, sub)]


def route(live_ref, dest_ref, heading_ref, misfit_ref, out_ref):
    tiles = out_ref.shape[0]
    own = misfit_ref.shape[0]
    dest = dest_ref[...]
    row_id = lax.broadcasted_iota(jnp.int32, (1, own), 1)
    live = row_id < live_ref[0]
    one = lax.broadcasted_iota(jnp.int32, (tiles, own), 0) == dest
    onehot = jnp.where(one, 1.0, 0.0)
    earlier = jnp.where(
        lax.broadcasted_iota(jnp.int32, (own, own), 0) < lax.broadcasted_iota(jnp.int32, (own, own), 1),
        1.0,
        0.0,
    ).astype(BF16)
    before = mm(onehot.astype(BF16), earlier)
    slot = jnp.sum(before * onehot, axis=0, keepdims=True).astype(jnp.int32)
    position = jnp.where(live, dest * 8 + slot, -1)
    angle = heading_ref[...]
    v_high, v_low = halves(misfit_ref[...])
    step = 256
    for first in range(0, tiles * 8, step):
        here = lax.broadcasted_iota(jnp.int32, (step, own), 0) + first == position
        for comp, factor in enumerate((jnp.cos(angle), jnp.sin(angle))):
            f_high, f_low = halves(factor)
            s_high = jnp.where(here, f_high.astype(F32), 0.0).astype(BF16)
            s_low = jnp.where(here, f_low.astype(F32), 0.0).astype(BF16)
            part = mm(s_high, v_high) + (mm(s_high, v_low) + mm(s_low, v_high))
            out_ref[first // 8 : (first + step) // 8, 8 * comp : 8 * comp + 8, :] = part.reshape(step // 8, 8, 128)


def scatter_group(rows8, cols8, values, acc_ref):
    largest = functools.reduce(jnp.maximum, [jnp.abs(v) for pair in values for v in pair])
    largest = jnp.maximum(jnp.max(largest, keepdims=True), 1e-30)
    scale, back = 384.0 / largest, largest * (1.0 / 384.0)
    left, right = [], []
    sub = 16
    zero = jnp.zeros((sub, 128), BF16)
    unit = jnp.ones((sub, 128), BF16)
    for rows, cols, pair in zip(rows8, cols8, values):
        pieces = []
        for v in pair:
            rest = v * scale
            for _ in range(PIECES):
                piece = rest.astype(BF16).astype(F8).astype(F32)
                pieces.append(piece)
                rest = (rest - piece) * 16.0
        for k in range(8):
            r = jnp.broadcast_to(rows[k : k + 1].astype(F32), (sub, 128)).astype(BF16)
            c = jnp.broadcast_to(cols[k : k + 1].astype(F32), (sub, 128)).astype(BF16)
            at_row = hot(r, 128, sub)
            wide = [jnp.broadcast_to(p[k : k + 1], (sub, 128)).astype(BF16) for p in pieces]
            left.append(jnp.concatenate([jnp.where(m, p, zero) for p in wide for m in at_row], axis=0).astype(F8))
            right.append(jnp.concatenate([jnp.where(m, unit, zero) for m in hot(c, 256, sub)], axis=0).astype(F8))
    acc_ref[...] += mm(jnp.concatenate(left, axis=1), jnp.concatenate(right, axis=1), NT) * back


def neighbours(gx, gy, n_gx, n_gy):
    found = []
    for dx in (-1, 0, 1):
        for dy in (-1, 0, 1):
            if dx or dy:
                found.append((dx, dy, lax.rem(gx + dx + n_gx, n_gx), lax.rem(gy + dy + n_gy, n_gy)))
    return found


def pack_rows(field):
    first = lax.broadcasted_iota(jnp.int32, (8, 256), 0) < 4
    return jnp.where(first, field[0:8], field[120:128])


def pack_cols(field):
    first = lax.broadcasted_iota(jnp.int32, (128, 128), 1) < 64
    return jnp.where(first, field[:, 0:128], field[:, 128:256])


def up(f):
    return pltpu.roll(f, f.shape[0] - 1, 0)


def down(f):
    return pltpu.roll(f, 1, 0)


def right(f):
    return pltpu.roll(f, f.shape[1] - 1, 1)


def left(f):
    return pltpu.roll(f, 1, 1)


def apply(e, n, eta, cx, cy, fric):
    e_up, e_right = up(e), right(e)
    n_up, n_right = up(n), right(n)
    ge = 0.5 * eta * (e_up - down(e))
    he = 0.5 * eta * (e_right - left(e))
    gn = 0.5 * eta * (n_up - down(n))
    hn = 0.5 * eta * (n_right - left(n))
    pe, qe = 4.0 * cx * (e_up - e), cy * (e_right - e)
    pn, qn = cx * (n_up - n), 4.0 * cy * (n_right - n)
    gn, he = 0.5 * gn, 0.5 * he
    out_e = down(pe + hn) - pe - up(hn) + left(qe + gn) - qe - right(gn) + fric * e
    out_n = down(pn + he) - pn - up(he) + left(qn + ge) - qn - right(ge) + fric * n
    return out_e, out_n


def fill_edges(ext, fields, flags, rows, cols, corners):
    top, bottom, west, east = flags
    has = lambda ok, value: jnp.where(ok, value, 0.0)
    both = jnp.logical_and
    for i, field in enumerate(fields):
        sub = lax.broadcasted_iota(jnp.int32, (8, 256), 0) < 4
        ext[field, 128:136, 0:256] = jnp.where(sub, has(bottom, rows[0, i]), has(top, rows[1, i]))
        sub = lax.broadcasted_iota(jnp.int32, (8, 128), 0) < 4
        first = jnp.where(sub, has(east, cols[0, i]), 0.0)
        last = jnp.where(sub, 0.0, has(west, cols[1, i]))
        turned = jnp.concatenate([first, jnp.zeros((112, 128), F32), last], axis=0)
        ext[field, 0:128, 256:384] = turned.T
        lane = lax.broadcasted_iota(jnp.int32, (8, 128), 1)
        sub = lax.broadcasted_iota(jnp.int32, (8, 128), 0) < 4
        below = jnp.where(lane < 64, has(both(bottom, east), corners[0, i]), has(both(bottom, west), corners[1, i]))
        above = jnp.where(lane < 64, has(both(top, east), corners[2, i]), has(both(top, west), corners[3, i]))
        value = jnp.where(sub, below, above)
        ext[field, 128:136, 256:384] = jnp.where((lane < 4) | (lane >= 124), value, 0.0)


def edge_copies(around, packed, got, sems):
    rows, cols, corner = packed
    got_rows, got_cols, got_corners = got
    copies = []
    for slot, (dx, dy, x, y) in enumerate(around):
        if dy == 0:
            src, dst = rows, got_rows.at[(dx + 1) // 2]
        elif dx == 0:
            src, dst = cols, got_cols.at[(dy + 1) // 2]
        else:
            src, dst = corner, got_corners.at[(dx + 1) + (dy + 1) // 2]
        copies.append(
            pltpu.make_async_remote_copy(
                src_ref=src,
                dst_ref=dst,
                send_sem=sems.at[0, slot],
                recv_sem=sems.at[1, slot],
                device_id=(x, y),
                device_id_type=MESH,
            )
        )
    return copies


def pack_edge(i, field, packed):
    rows, cols, corner = packed
    rows[i] = pack_rows(field)
    edge = pack_cols(field)
    turned = edge.T
    first = lax.broadcasted_iota(jnp.int32, (8, 128), 0) < 4
    cols[i] = jnp.where(first, turned[0:8], turned[120:128])
    corner[i] = jnp.where(first, edge[0:8], edge[120:128])


def body(
    n_gx,
    n_gy,
    live_ref,
    dest_hbm,
    heading_hbm,
    misfit_hbm,
    start_hbm,
    visc_hbm,
    fric_hbm,
    mask_hbm,
    lists_hbm,
    ice_ref,
    dest_ref,
    heading_ref,
    misfit_ref,
    start_ref,
    visc_ref,
    fric_ref,
    mask_ref,
    lists,
    outgoing,
    arrived,
    acc,
    ext,
    fixed_rows,
    fixed_cols,
    fixed_corner,
    fixed_got_rows,
    fixed_got_cols,
    fixed_got_corners,
    load_rows,
    load_cols,
    load_corner,
    load_got_rows,
    load_got_cols,
    load_got_corners,
    in_sems,
    send_sem,
    recv_sem,
    fixed_sems,
    load_sems,
    all_sem,
):
    gx, gy = lax.axis_index("gx"), lax.axis_index("gy")
    me = gx * n_gy + gy
    around = neighbours(gx, gy, n_gx, n_gy)
    loads = [
        pltpu.make_async_copy(src, dst, in_sems.at[i])
        for i, (src, dst) in enumerate(
            [
                (dest_hbm, dest_ref),
                (heading_hbm, heading_ref),
                (misfit_hbm, misfit_ref),
                (start_hbm, start_ref),
                (visc_hbm, visc_ref),
                (fric_hbm, fric_ref),
                (mask_hbm, mask_ref),
                (lists_hbm, lists),
            ]
        )
    ]
    for copy in loads:
        copy.start()

    barrier = pltpu.get_barrier_semaphore()
    for a in range(1, n_gx):
        pl.semaphore_signal(barrier, inc=1, device_id=(lax.rem(gx + a, n_gx), gy), device_id_type=MESH)
    for b in range(1, n_gy):
        pl.semaphore_signal(barrier, inc=1, device_id=(gx, lax.rem(gy + b, n_gy)), device_id_type=MESH)

    for copy in loads[0:3]:
        copy.wait()
    route(live_ref, dest_ref, heading_ref, misfit_ref, outgoing)
    acc[...] = jnp.zeros_like(acc)
    fixed_packed = (fixed_rows, fixed_cols, fixed_corner)

    pl.semaphore_wait(barrier, n_gx + n_gy - 2)
    fixed_got = (fixed_got_rows, fixed_got_cols, fixed_got_corners)
    fixed_copies = edge_copies(around, fixed_packed, fixed_got, fixed_sems)

    def send_group(g, first=0):
        y = lax.rem(gy + g, n_gy)
        for a in range(first, n_gx):
            x = lax.rem(gx + a, n_gx)
            pltpu.make_async_remote_copy(
                src_ref=outgoing.at[x * n_gy + y],
                dst_ref=arrived.at[gy, gx],
                send_sem=send_sem,
                recv_sem=recv_sem.at[g],
                device_id=(x, y),
                device_id_type=MESH,
            ).start()

    pltpu.make_async_copy(outgoing.at[me], arrived.at[gy, gx], recv_sem.at[0]).start()
    send_group(0, 1)
    for b in range(1, n_gy):
        pl.semaphore_signal(
            all_sem.at[b], inc=1, device_id=(gx, lax.rem(gy + n_gy - b, n_gy)), device_id_type=MESH
        )

    def send_next(g, carry):
        pl.semaphore_wait(all_sem.at[g], 1)
        send_group(g)
        return carry

    lax.fori_loop(1, AHEAD, send_next, 0)
    for copy in loads[3:7]:
        copy.wait()
    fields = [start_ref[0], start_ref[1], visc_ref[...], fric_ref[...], mask_ref[...].astype(F32)]
    for i, f in enumerate(fields):
        ext[2 + i, 0:128, 0:256] = f
        pack_edge(i, f, fixed_packed)
    for copy in loads[7:8]:
        copy.wait()

    def take_group(g):
        y = lax.rem(gy + n_gy - g, n_gy)
        pltpu.make_async_copy(outgoing.at[0:n_gx], arrived.at[y], recv_sem.at[g]).wait()
        sources = [x * n_gy + y for x in range(n_gx)]
        scatter_group(
            [lists[s, :, 0, :] for s in sources],
            [lists[s, :, 1, :] for s in sources],
            [(arrived[y, x, 0:8, :], arrived[y, x, 8:16, :]) for x in range(n_gx)],
            acc,
        )

    def send_and_take(g, carry):
        send_next(g + AHEAD, carry)
        take_group(g)
        return carry

    def take(g, carry):
        take_group(g)
        return carry

    lax.fori_loop(0, n_gy - AHEAD, send_and_take, 0)
    for copy in fixed_copies:
        copy.start()
    lax.fori_loop(n_gy - AHEAD, n_gy, take, 0)

    load_packed = (load_rows, load_cols, load_corner)
    for i in range(2):
        parts = [acc[128 * (PIECES * i + p) : 128 * (PIECES * i + p + 1)] for p in range(PIECES)]
        f = parts[0] + (parts[1] + parts[2] * (1.0 / 16.0)) * (1.0 / 16.0)
        ext[i, 0:128, 0:256] = f
        pack_edge(i, f, load_packed)
    load_got = (load_got_rows, load_got_cols, load_got_corners)
    load_copies = edge_copies(around, load_packed, load_got, load_sems)
    for copy in load_copies:
        copy.start()

    for copy in fixed_copies:
        copy.wait_recv()
    flags = (gx > 0, gx < n_gx - 1, gy > 0, gy < n_gy - 1)
    fill_edges(ext, range(2, 7), flags, *fixed_got)
    eta, fric, mask = ext[4], ext[5], ext[6]
    ext[7], ext[8] = 0.5 * (eta + up(eta)), 0.5 * (eta + right(eta))
    ext[9] = TAU * mask
    ext[2] = mask * ext[2]
    ext[3] = mask * ext[3]
    out_e, out_n = apply(ext[2], ext[3], ext[4], ext[7], ext[8], ext[5])
    ext[2] = ext[2] - ext[9] * out_e
    ext[3] = ext[3] - ext[9] * out_n

    for copy in load_copies:
        copy.wait_recv()
    fill_edges(ext, range(2), flags, *load_got)
    ext[0] = ext[9] * ext[0]
    ext[1] = ext[9] * ext[1]
    ext[2] = ext[2] + ext[0]
    ext[3] = ext[3] + ext[1]

    def sweep(_, carry):
        out_e, out_n = apply(ext[2], ext[3], ext[4], ext[7], ext[8], ext[5])
        ext[2] = ext[2] + (ext[0] - ext[9] * out_e)
        ext[3] = ext[3] + (ext[1] - ext[9] * out_n)
        return carry

    lax.fori_loop(0, ITERS - 1, sweep, 0)
    ice_ref[...] = ext[2:4, 0:128, 0:256]

    for copy in fixed_copies + load_copies:
        copy.wait_send()
    sent = n_gx * n_gy - 1
    pltpu.make_async_remote_copy(
        src_ref=outgoing.at[0:sent],
        dst_ref=outgoing.at[0:sent],
        send_sem=send_sem,
        recv_sem=recv_sem.at[0],
        device_id=(gx, gy),
        device_id_type=MESH,
    ).wait_send()


def finish(
    ice_hbm, start_hbm, fric_hbm, mask_hbm, vel_hbm, adj_hbm, grad_hbm, ice_ref, start_ref, fric_ref, mask_ref, vel_ref, adj_ref, grad_ref, sems
):
    pairs = [(ice_hbm, ice_ref), (start_hbm, start_ref), (mask_hbm, mask_ref), (fric_hbm, fric_ref), (vel_hbm, vel_ref)]
    loads = [pltpu.make_async_copy(src, dst, sems.at[i]) for i, (src, dst) in enumerate(pairs)]
    for copy in loads:
        copy.start()
    for copy in loads[0:3]:
        copy.wait()
    here = mask_ref[...] > 0
    keep = (1.0 - TAU) ** ITERS
    adj_ref[0] = jnp.where(here, ice_ref[0], keep * start_ref[0])
    adj_ref[1] = jnp.where(here, ice_ref[1], keep * start_ref[1])
    adj_copy = pltpu.make_async_copy(adj_ref, adj_hbm, sems.at[5])
    adj_copy.start()
    for copy in loads[3:5]:
        copy.wait()
    grad_ref[...] = -(fric_ref[...] * (vel_ref[0] * ice_ref[0] + vel_ref[1] * ice_ref[1]))
    grad_copy = pltpu.make_async_copy(grad_ref, grad_hbm, sems.at[6])
    grad_copy.start()
    adj_copy.wait()
    grad_copy.wait()


VMEM = pl.BlockSpec(memory_space=pltpu.VMEM)
SMEM = pl.BlockSpec(memory_space=pltpu.SMEM)
HBM = pl.BlockSpec(memory_space=pltpu.HBM)


def edge_scratch(fields):
    return [
        pltpu.VMEM((fields, 8, 256), F32),
        pltpu.VMEM((fields, 8, 128), F32),
        pltpu.VMEM((fields, 8, 128), F32),
        pltpu.VMEM((2, fields, 8, 256), F32),
        pltpu.VMEM((2, fields, 8, 128), F32),
        pltpu.VMEM((4, fields, 8, 128), F32),
    ]


def shards(n_gx, n_gy, start, velocity, viscosity, friction, ice_mask, misfit, heading, row_dest, live_rows, lists):
    tiles = n_gx * n_gy
    own = misfit.shape[0]
    on_ice = pl.pallas_call(
        functools.partial(body, n_gx, n_gy),
        out_shape=jax.ShapeDtypeStruct((2, 128, 256), F32),
        in_specs=[SMEM] + [HBM] * 8,
        out_specs=VMEM,
        scratch_shapes=[
            pltpu.VMEM((1, own), jnp.int32),
            pltpu.VMEM((1, own), F32),
            pltpu.VMEM(misfit.shape, F32),
            pltpu.VMEM(start.shape, F32),
            pltpu.VMEM(viscosity.shape, F32),
            pltpu.VMEM(friction.shape, F32),
            pltpu.VMEM(ice_mask.shape, jnp.int32),
            pltpu.VMEM(lists.shape, jnp.int32),
            pltpu.VMEM((tiles, 16, 128), F32),
            pltpu.VMEM((n_gy, n_gx, 16, 128), F32),
            pltpu.VMEM((2 * PIECES * 128, 256), F32),
            pltpu.VMEM((10, 136, 384), F32),
            *edge_scratch(5),
            *edge_scratch(2),
            pltpu.SemaphoreType.DMA((8,)),
            pltpu.SemaphoreType.DMA,
            pltpu.SemaphoreType.DMA((n_gy,)),
            pltpu.SemaphoreType.DMA((2, 8)),
            pltpu.SemaphoreType.DMA((2, 8)),
            pltpu.SemaphoreType.REGULAR((n_gy,)),
        ],
        compiler_params=pltpu.CompilerParams(collective_id=0, has_side_effects=True, vmem_limit_bytes=60 << 20),
        name="shelf",
    )(
        live_rows,
        row_dest.reshape(1, own),
        heading.reshape(1, own),
        misfit,
        start,
        viscosity,
        friction,
        ice_mask,
        lists,
    )
    return pl.pallas_call(
        finish,
        out_shape=(jax.ShapeDtypeStruct((2, 128, 256), F32), jax.ShapeDtypeStruct((128, 256), F32)),
        in_specs=[HBM] * 5,
        out_specs=(HBM, HBM),
        scratch_shapes=[
            pltpu.VMEM((2, 128, 256), F32),
            pltpu.VMEM((2, 128, 256), F32),
            pltpu.VMEM((128, 256), F32),
            pltpu.VMEM((128, 256), jnp.int32),
            pltpu.VMEM((2, 128, 256), F32),
            pltpu.VMEM((2, 128, 256), F32),
            pltpu.VMEM((128, 256), F32),
            pltpu.SemaphoreType.DMA((7,)),
        ],
        compiler_params=pltpu.CompilerParams(vmem_limit_bytes=60 << 20),
        name="finish",
    )(on_ice, start, friction, ice_mask, velocity)


def solution(mesh):
    in_specs = (
        P(None, "gx", "gy"),
        P(None, "gx", "gy"),
        P("gx", "gy"),
        P("gx", "gy"),
        P("gx", "gy"),
        P(("gx", "gy"), None),
        P(("gx", "gy")),
        P(("gx", "gy"), None),
        P(("gx", "gy")),
        P(("gx", "gy"), None, None, None),
    )
    return jax.shard_map(
        functools.partial(shards, mesh.shape["gx"], mesh.shape["gy"]),
        mesh=mesh,
        in_specs=in_specs,
        out_specs=(P(None, "gx", "gy"), P("gx", "gy")),
        check_vma=False,
    )
```
